128 devices in a mesh: group: 16 (over x, z), inner: 8 (over y, core).
Axes of the slice: x: 4, y: 4, z: 4, core: 2. Of those that a mesh axis runs over, the one named last changes fastest.
Arguments:
- densities: float32 [1024, 64, 64], P('group'), may hold values from -1 to 2, as said below
- ref_charge: float32 [1024, 16], P('group'), may hold values from 2.1 to 3.1
- site_pos: float32 [3, 16384], P(None, 'group'), may hold values from 0 to 48
- dimer_pairs: int32 [256, 2], replicated, may hold values from 0 to 1023, as said below
- probe_pos: float32 [3, 2048], P(None, ('group', 'inner')), may hold values from 0 to 48
- core_ham: float32 [256, 128, 128], P(('group', 'inner')), may hold values from -4 to 4
- probe_ints: bfloat16 [256, 8, 128, 128], P(('group', 'inner')), may hold values from -0.375 to 0.375
- ri_ints: bfloat16 [256, 256, 128, 128], P(('group', 'inner')), may hold values from -0.1875 to 0.1875
Outputs:
- frag_weight: float32 [1024, 64, 64], P('group', 'inner')
- dimer_energy: float32 [256], P(('group', 'inner'))
The draws below stay inside these ranges and needn't reach their ends.
Inputs may be any that keep to these rules, and one draw needn't show every extreme that they name: `densities`: symmetric in the last two dimensions. `dimer_pairs`: the two fragments of a dimer differ; within the 16 rows of one group no fragment appears twice, and at most 4 of them lie in the block of 64 fragments owned by one group. In every draw one owning group gives exactly 4 fragments to every group.
All inputs are finite; a program needn't handle non-finite values.
Results may differ from the reference program's by a relative error of at most 0.0035.
Values sent between devices are 32-bit elements; how exact they have to be, the bound alone decides.
No kernel may reach another device: no remote copies, remote signals or barrier semaphores. Data moves between devices by JAX's collectives and lax.ppermute only.
A program may use at most 128 MiB of HBM per device.

```python
import math
import jax
import jax.numpy as jnp
from jax import lax

NB = 64
NB2 = 128
NAUX = 256
ATOMS = 16
NPROBE = 8
ITERS = 3
FRAG_GRP = 64
DIM_GRP = 16
DIMERS = 256
FRAGS = 1024
SITES = 16384
CAP = 4
N_GROUP = 16


def pair_table(key):
    key = jax.random.fold_in(key, 11)
    hot_owner = jax.random.randint(jax.random.fold_in(key, 1), (), 0, N_GROUP)
    rest_count = 2 * DIM_GRP - CAP

    def one_group(group_id):
        group_key = jax.random.fold_in(key, group_id + 2)
        order = jax.random.permutation(jax.random.fold_in(group_key, 0), (N_GROUP - 1) * CAP)[:rest_count]
        owners = jnp.concatenate([jnp.zeros((CAP,), jnp.int32) + hot_owner, (hot_owner + 1 + order // CAP) % N_GROUP]).astype(jnp.int32)
        ranks = jnp.concatenate([jnp.arange(CAP, dtype=jnp.int32), (order % CAP).astype(jnp.int32)])
        tables = jax.vmap(lambda owner_id: jax.random.permutation(jax.random.fold_in(group_key, owner_id + 1), FRAG_GRP))(jnp.arange(N_GROUP))
        local_ids = tables[owners, ranks].astype(jnp.int32)
        frag_ids = owners * FRAG_GRP + local_ids
        shuffle = jax.random.permutation(jax.random.fold_in(group_key, N_GROUP + 5), 2 * DIM_GRP)
        return frag_ids[shuffle].reshape(DIM_GRP, 2)
    groups = jax.vmap(one_group)(jnp.arange(N_GROUP, dtype=jnp.int32))
    return groups.reshape(DIMERS, 2).astype(jnp.int32)


def box_upper():
    depth = 3.0 * FRAGS / 64.0
    return jnp.array([24.0, 24.0, depth], jnp.float32)


def fragment_centres(key):
    key = jax.random.fold_in(key, 23)
    depth = 3.0 * FRAGS / 64.0
    lower = jnp.array([0.6, 0.6, 0.6], jnp.float32)
    upper = jnp.array([23.4, 23.4, depth - 0.6], jnp.float32)
    unit = jax.random.uniform(key, (3, FRAGS), jnp.float32)
    return lower[:, None] + unit * (upper - lower)[:, None]


def draw_densities(key, part):
    key = jax.random.fold_in(key, 5)
    noise_key = jax.random.fold_in(key, 1)
    diag_key = jax.random.fold_in(key, 2)
    noise = jnp.clip(jax.random.normal(noise_key, (FRAGS, NB, NB), jnp.float32), -4.0, 4.0)
    noise = noise * (0.5 / math.sqrt(NB))
    symmetric = 0.5 * (noise + jnp.swapaxes(noise, 1, 2))
    diagonal = jax.random.uniform(diag_key, (FRAGS, NB), jnp.float32, 0.3, 1.0)
    return symmetric + diagonal[:, :, None] * jnp.eye(NB, dtype=jnp.float32)[None, :, :]


def draw_dimer_pairs(key, part):
    return pair_table(key)


def draw_site_pos(key, part):
    centres = fragment_centres(key)
    key = jax.random.fold_in(key, 31)
    offsets = jax.random.uniform(key, (3, FRAGS, ATOMS), jnp.float32, -8.0, 8.0)
    placed = centres[:, :, None] + offsets
    placed = jnp.clip(placed, 0.0, box_upper()[:, None, None])
    return placed.reshape(3, SITES)


def draw_probe_pos(key, part):
    pairs = pair_table(key)
    centres = fragment_centres(key)
    key = jax.random.fold_in(key, 37)
    which = (jnp.arange(NPROBE, dtype=jnp.int32) >= NPROBE // 2).astype(jnp.int32)
    frag_of_probe = jnp.where(which[None, :] == 1, pairs[:, 1:2], pairs[:, 0:1])
    near = centres[:, frag_of_probe]
    offsets = jax.random.uniform(key, (3, DIMERS, NPROBE), jnp.float32, -3.0, 3.0)
    placed = jnp.clip(near + offsets, 0.0, box_upper()[:, None, None])
    return placed.reshape(3, DIMERS * NPROBE)


def block_levels(own_key, dims, pieces, smallest, high):
    loudness, own = 1.0, jax.random.fold_in(own_key, 6)
    for position, blocks in pieces:
        steps = jnp.exp(jax.random.uniform(jax.random.fold_in(own, position), (blocks,), jnp.float32, smallest / len(pieces), high / len(pieces)))
        loudness = loudness * jnp.repeat(steps, dims[position] // blocks).reshape([-1 if axis == position else 1 for axis in range(len(dims))])
    return loudness


def centred(rng, shape, deviation, limit, shards=(), kind=jnp.bfloat16):
    values = deviation * jax.random.normal(rng, shape, jnp.float32)
    if shards:
        values = values * block_levels(rng, shape, shards, -0.22, 0.18)
    return jnp.clip(values, -limit, limit).astype(kind)


def setup_inputs(seed: int = 0) -> dict:
    key_list = jax.random.split(jax.random.key(seed), 9)
    densities = draw_densities(jax.random.fold_in(key_list[8], 71), 0)
    ref_charge = jnp.clip(2.1 + 1.0 * jax.random.uniform(key_list[1], (FRAGS, ATOMS), jnp.float32) ** block_levels(key_list[1], (FRAGS, ATOMS), ((0, 16),), -0.2, 0.2), 2.1, 3.1)
    site_pos = draw_site_pos(jax.random.fold_in(key_list[8], 71), 0)
    dimer_pairs = draw_dimer_pairs(jax.random.fold_in(key_list[8], 71), 0)
    probe_pos = draw_probe_pos(jax.random.fold_in(key_list[8], 71), 0)
    core_ham = centred(key_list[5], (DIMERS, NB2, NB2), 0.5, 4.0, ((0, 128),), jnp.float32)
    probe_ints = centred(key_list[6], (DIMERS, NPROBE, NB2, NB2), (2 * NPROBE * ATOMS) ** -0.5, 0.375, ((0, 128),))
    ri_ints = centred(key_list[7], (DIMERS, NAUX, NB2, NB2), (NB2 * NB2 // 16) ** -0.5, 0.1875, ((0, 128),))
    return {"densities": densities, "ref_charge": ref_charge, "site_pos": site_pos, "dimer_pairs": dimer_pairs, "probe_pos": probe_pos, "core_ham": core_ham, "probe_ints": probe_ints, "ri_ints": ri_ints}


damping = 0.1
highest = lax.Precision.HIGHEST

def site_charges(densities, ref_charge):
    nbasis = densities.shape[1]
    diagonal = jnp.diagonal(densities, axis1=1, axis2=2)
    per_atom = lax.optimization_barrier(jnp.sum(diagonal.reshape(diagonal.shape[0], ATOMS, nbasis // ATOMS), axis=2))
    return (ref_charge - per_atom).reshape(-1)

def field_weights(probes, positions, charges, site_frag, first, second):
    offsets = probes[:, :, None] - positions[:, None, :]
    kernel = lax.rsqrt(lax.optimization_barrier(jnp.sum(offsets * offsets, axis=0)) + 1.0)
    keep_mask = jnp.logical_and(site_frag != first, site_frag != second).astype(jnp.float32)
    return lax.optimization_barrier(jnp.sum(kernel * (keep_mask * charges)[None, :], axis=1))

def block_start(first_block, second_block):
    zero_block = jnp.zeros_like(first_block)
    upper_rows = jnp.concatenate([first_block, zero_block], axis=1)
    lower_rows = jnp.concatenate([zero_block, second_block], axis=1)
    return jnp.concatenate([upper_rows, lower_rows], axis=0)

def to_half(values):
    return lax.optimization_barrier(values.astype(jnp.bfloat16)).astype(jnp.float32)

def dimer_scf(ri_block, probe_block, core_block, weights, start):
    nbasis2 = start.shape[0]
    potential = jnp.einsum('k,kmn->mn', weights, probe_block.astype(jnp.float32), precision=highest)
    fixed_part = core_block + potential
    ri_wide = ri_block.astype(jnp.float32)
    density = start
    fock_matrix = fixed_part
    for sweep in range(ITERS):
        packed = to_half(density)
        fit_coef = to_half(jnp.einsum('qmn,mn->q', ri_wide, packed, precision=highest))
        coulomb = jnp.einsum('q,qmn->mn', fit_coef, ri_wide, precision=highest)
        half_product = to_half(jnp.einsum('qml,ln->qmn', ri_wide, packed, precision=highest))
        exch_matrix = jnp.einsum('qml,qln->mn', half_product, ri_wide, precision=highest)
        fock_matrix = fixed_part + coulomb - 0.5 * exch_matrix
        moved = jnp.dot(jnp.dot(start, fock_matrix, precision=highest), start, precision=highest)
        density = start - damping * moved
    weighted = jnp.dot(jnp.dot(density, fock_matrix, precision=highest), density, precision=highest)
    energy = 0.5 * jnp.sum(density * (core_block + fock_matrix)) / nbasis2
    return (energy, weighted)

def reference(densities, ref_charge, site_pos, dimer_pairs, probe_pos, core_ham, probe_ints, ri_ints):
    charges = site_charges(densities, ref_charge)
    site_frag = jnp.arange(SITES, dtype=jnp.int32) // ATOMS

    def one_dimer(parts):
        index, ri_block, probe_block, core_block = parts
        first = dimer_pairs[index, 0]
        second = dimer_pairs[index, 1]
        probes = lax.dynamic_slice_in_dim(probe_pos, index * NPROBE, NPROBE, 1)
        weights = field_weights(probes, site_pos, charges, site_frag, first, second)
        start = block_start(densities[first], densities[second])
        energy, weighted = dimer_scf(ri_block, probe_block, core_block, weights, start)
        return (energy, weighted[:NB, :NB], weighted[NB:, NB:])
    energy, first_weight, second_weight = lax.map(one_dimer, (jnp.arange(DIMERS, dtype=jnp.int32), ri_ints, probe_ints, core_ham))
    frag_weight = jnp.zeros((FRAGS, NB, NB), jnp.float32)
    frag_weight = frag_weight.at[dimer_pairs[:, 0]].add(first_weight)
    frag_weight = frag_weight.at[dimer_pairs[:, 1]].add(second_weight)
    return (frag_weight, energy)
```

```python
import jax
import jax.numpy as jnp
from jax import lax
from jax.experimental import pallas as pl
from jax.experimental.pallas import tpu as pltpu
from jax.sharding import PartitionSpec as P

NB = 64
NB2 = 128
NAUX = 256
ATOMS = 16
NPROBE = 8
ITERS = 3
FRAG_GRP = 64
DIM_GRP = 16
CAP = 4
N_GROUP = 16
N_Y = 4
SITE_ROWS = 8
HALF = SITE_ROWS // 2
ROWS = NB + 4 * HALF
STRIDE = 8

STEP = 64
PART = 4
CHUNKS = 4

damping = 0.1
highest = lax.Precision.HIGHEST
VMEM = pl.BlockSpec(memory_space=pltpu.VMEM)
SMEM = pl.BlockSpec(memory_space=pltpu.SMEM)
ANY = pl.BlockSpec(memory_space=pl.ANY)


def dot32(a, b):
    return jnp.dot(a, b, precision=highest, preferred_element_type=jnp.float32)


def iota(shape, dim):
    return lax.broadcasted_iota(jnp.int32, shape, dim)


def endpoint(pairs, group, e):
    return pairs[e % 2, group * DIM_GRP + e // 2]


def owner_of(frag):
    return lax.shift_right_logical(frag, 6)


def pack_kernel(pos, pairs, dens_hbm, ref_charge, site_pos, send, table, dens, sem):
    group, core = pos[0], pos[2]
    load = pltpu.make_async_copy(dens_hbm, dens, sem)
    load.start()

    def list_group(g, carry):
        count = jnp.int32(0)
        for e in range(2 * DIM_GRP):
            frag = endpoint(pairs, g, e)
            table[g * STRIDE + count] = lax.bitwise_and(frag, FRAG_GRP - 1)
            count = count + (owner_of(frag) == group).astype(jnp.int32)
        table[g * STRIDE + STRIDE - 1] = count
        return carry

    lax.fori_loop(0, N_GROUP, list_group, 0)
    load.wait()

    eye = iota((NB, NB), 0) == iota((NB, NB), 1)
    diagonal = jnp.sum(jnp.where(eye[None], dens[...], 0.0), axis=1)
    spread = (iota((NB, 128), 0) // (NB // ATOMS) == iota((NB, 128), 1) % ATOMS).astype(jnp.float32)
    repeat = (iota((ATOMS, 128), 0) == iota((ATOMS, 128), 1) % ATOMS).astype(jnp.float32)
    charge = dot32(ref_charge[...], repeat) - dot32(diagonal, spread)
    mine = iota((FRAG_GRP, 128), 0) % (128 // ATOMS) == iota((FRAG_GRP, 128), 1) // ATOMS
    charge = jnp.sum(jnp.where(mine, charge, 0.0).reshape(SITE_ROWS, 128 // ATOMS, 128), axis=1)

    def half_of(rows):
        return jnp.where(core == 0, rows[:HALF], rows[HALF:])

    sites = jnp.concatenate([half_of(site_pos[c]) for c in range(3)] + [half_of(charge)], axis=0)

    def fill(g, carry):
        count = table[g * STRIDE + STRIDE - 1]
        pair = []
        for s in range(2):
            slot = 2 * core + s
            pair.append(dens[jnp.where(slot < count, table[g * STRIDE + slot], 0)])
        send[g, :NB] = jnp.concatenate(pair, axis=1)
        send[g, NB:] = sites
        return carry

    lax.fori_loop(0, N_GROUP, fill, 0)


def scf_kernel(pos, pairs, probe_pos, mine, other, core_ham, probe_ints, ri_hbm,
               keep, give, energy, ri, start, fixed, dens, packed, fock, weighted, sems):
    group, chip, core = pos[0], pos[1], pos[2]
    steps = NAUX // STEP
    per_chunk = NAUX // CHUNKS

    def load(c):
        part = pl.ds(c * per_chunk, per_chunk)
        return pltpu.make_async_copy(ri_hbm.at[:, part], ri.at[:, part], sems.at[c])

    for c in range(CHUNKS):
        load(c).start()

    first_dimer = (2 * chip + core) * 2
    left = iota((NB, NB2), 1) < NB

    def fragment_rows(dimer, side):
        e = 2 * dimer + side
        owner = owner_of(pairs[side, group * DIM_GRP + dimer])
        rank = jnp.int32(0)
        for k in range(2 * DIM_GRP):
            hit = jnp.logical_and(owner_of(endpoint(pairs, group, k)) == owner, k < e)
            rank = rank + hit.astype(jnp.int32)
        rows = jnp.where(rank // 2 == core, mine[owner, :NB], other[owner, :NB])
        return jnp.where(rank % 2 == side, rows, pltpu.roll(rows, NB, 1))

    for d in range(2):
        start[d, :NB] = jnp.where(left, fragment_rows(first_dimer + d, 0), 0.0)
        start[d, NB:] = jnp.where(left, 0.0, fragment_rows(first_dimer + d, 1))
        dens[d] = start[d]

    def gathered(c):
        rows = slice(NB + HALF * c, NB + HALF * (c + 1))
        return jnp.concatenate([mine[:, rows], other[:, rows]], axis=1)

    xs, ys, zs, charge = (gathered(c) for c in range(4))
    shape = (N_GROUP, SITE_ROWS, 128)
    row = iota(shape, 1)
    row = jnp.where(row < HALF, row + HALF * core, row - HALF * core)
    site_frag = iota(shape, 0) * FRAG_GRP + row * (128 // ATOMS) + iota(shape, 2) // ATOMS
    for d in range(2):
        column = group * DIM_GRP + first_dimer + d
        keep_site = jnp.logical_and(site_frag != pairs[0, column], site_frag != pairs[1, column])
        kept = jnp.where(keep_site, charge, 0.0)
        total = core_ham[d]
        for k in range(NPROBE):
            at = d * NPROBE + k
            dx, dy, dz = xs - probe_pos[0, at], ys - probe_pos[1, at], zs - probe_pos[2, at]
            terms = kept * lax.rsqrt(dx * dx + dy * dy + dz * dz + 1.0)
            weight = jnp.sum(jnp.sum(terms, axis=0), axis=(0, 1), keepdims=True)
            total = total + weight * probe_ints[d, k].astype(jnp.float32)
        fixed[d] = total

    eye = iota((NB2, NB2), 0) == iota((NB2, NB2), 1)
    zero = jnp.zeros((NB2, NB2), jnp.bfloat16)

    def accumulate(step):
        both = jnp.concatenate([jnp.concatenate([packed[0], zero], axis=1),
                                jnp.concatenate([zero, packed[1]], axis=1)], axis=0)
        sums = [fock[0], fock[1]]
        for g in range(STEP // PART):
            at = pl.ds(step * STEP + g * PART, PART)
            parts = [ri[d, at] for d in range(2)]
            wide = jnp.concatenate([p.reshape(PART * NB2, NB2) for p in parts], axis=1)
            half = jnp.dot(wide, both, preferred_element_type=jnp.float32)
            rows = []
            for d in range(2):
                blocks = []
                for i in range(PART):
                    block = half[i * NB2:(i + 1) * NB2, d * NB2:(d + 1) * NB2]
                    fit = (parts[d][i] * packed[d]).astype(jnp.float32).reshape(-1, 8, NB2)
                    fit = jnp.sum(jnp.sum(fit, axis=0), axis=(0, 1), keepdims=True)
                    fit = -2.0 * fit.astype(jnp.bfloat16).astype(jnp.float32)
                    blocks.append(jnp.where(eye, block + fit, block).astype(jnp.bfloat16))
                rows.append(jnp.concatenate(blocks, axis=1))
            out = jnp.dot(jnp.concatenate(rows, axis=0), wide, preferred_element_type=jnp.float32)
            sums[0] = sums[0] + out[:NB2, :NB2]
            sums[1] = sums[1] + out[NB2:, NB2:]
        fock[0] = sums[0]
        fock[1] = sums[1]

    def sweep(t, carry):
        packed[...] = dens[...].astype(jnp.bfloat16)
        fock[...] = jnp.zeros_like(fock)

        def body(step, inner_carry):
            @pl.when(t == 0)
            def _():
                load(step).wait()

            accumulate(step)
            return inner_carry

        lax.fori_loop(0, steps, body, 0)
        for d in range(2):
            matrix = fixed[d] - 0.5 * fock[d]
            fock[d] = matrix
            dens[d] = start[d] - damping * dot32(dot32(start[d], matrix), start[d])
        return carry

    lax.fori_loop(0, ITERS, sweep, 0)

    for d in range(2):
        matrix, density = fock[d], dens[d]
        energy[d] = (0.5 / NB2) * jnp.sum(density * (core_ham[d] + matrix))
        block = dot32(dot32(density, matrix), density)
        weighted[d] = jnp.where(left, block[:NB], block[NB:])
    for k in range(N_Y):
        for d in range(2):
            rows = 2 * lax.rem(chip + k, N_Y)
            keep[k, d] = weighted[d, pl.ds(pl.multiple_of((rows + core) * 8, 8), 8)]
            give[k, d] = weighted[d, pl.ds(pl.multiple_of((rows + 1 - core) * 8, 8), 8)]


def route_kernel(pos, pairs, own0, own1, got1, got2, got3, out, count, owners, ranks):
    group, chip, core = pos[0], pos[1], pos[2]
    for o in range(N_GROUP):
        count[o] = 0
    for e in range(2 * DIM_GRP):
        owner = owner_of(endpoint(pairs, group, e))
        rank = count[owner]
        owners[e] = owner
        ranks[e] = rank
        count[owner] = rank + 1
    out[...] = jnp.zeros_like(out)
    lane_half = iota((8, 128), 1) // NB
    for k in range(N_Y):
        for src in range(2):
            for d in range(2):
                if k == 0:
                    block = (own0, own1)[src][d]
                else:
                    block = (got1, got2, got3)[k - 1][src, d]
                turned = pltpu.roll(block, NB, 1)
                from_core = core if src == 0 else 1 - core
                dimer = (2 * lax.rem(chip - k + N_Y, N_Y) + from_core) * 2 + d
                for side in range(2):
                    owner, rank = owners[2 * dimer + side], ranks[2 * dimer + side]
                    half = lax.rem(rank, 2)
                    value = jnp.where(half == side, block, turned)
                    here = (owner, lax.div(rank, 2))
                    out[here] = jnp.where(lane_half == half, value, out[here])


def home_kernel(table, got, out):
    out[...] = jnp.zeros_like(out)

    def add(g, carry):
        count = table[g * STRIDE + STRIDE - 1]
        for s in range(CAP):
            at = jnp.where(s < count, table[g * STRIDE + s], 0)
            block = got[g, s // 2]
            value = block[:, :NB] if s % 2 == 0 else pltpu.roll(block, NB, 1)[:, :NB]
            out[at] = out[at] + jnp.where(s < count, value, 0.0)
        return carry

    lax.fori_loop(0, N_GROUP, add, 0)


def params(mib):
    return pltpu.CompilerParams(vmem_limit_bytes=mib * 1024 * 1024)


def per_device(densities, ref_charge, site_pos, dimer_pairs, probe_pos, core_ham, probe_ints, ri_ints):
    f32, i32 = jnp.float32, jnp.int32
    inner = lax.axis_index("inner")
    pos = jnp.stack([lax.axis_index("group"), inner // 2, inner % 2]).astype(i32)
    pairs = dimer_pairs.T
    n_inner = 2 * N_Y
    swap = [(i, i ^ 1) for i in range(n_inner)]

    with jax.named_scope("pack"):
        send, table = pl.pallas_call(
            pack_kernel,
            out_shape=(jax.ShapeDtypeStruct((N_GROUP, ROWS, 128), f32),
                       jax.ShapeDtypeStruct((N_GROUP * STRIDE,), i32)),
            in_specs=[SMEM, SMEM, ANY, VMEM, VMEM],
            out_specs=(VMEM, SMEM),
            scratch_shapes=[pltpu.VMEM((FRAG_GRP, NB, NB), f32), pltpu.SemaphoreType.DMA],
            compiler_params=params(16),
            name="pack",
        )(pos, pairs, densities, ref_charge, site_pos.reshape(3, SITE_ROWS, 128))
    mine = lax.all_to_all(send, "group", split_axis=0, concat_axis=0, tiled=True)
    other = lax.ppermute(mine, "inner", swap)

    with jax.named_scope("scf"):
        piece = jax.ShapeDtypeStruct((N_Y, 2, 8, 128), f32)
        square = pltpu.VMEM((2, NB2, NB2), f32)
        keep, give, energy = pl.pallas_call(
            scf_kernel,
            out_shape=(piece, piece, jax.ShapeDtypeStruct((2,), f32)),
            in_specs=[SMEM, SMEM, SMEM, VMEM, VMEM, VMEM, VMEM, ANY],
            out_specs=(VMEM, VMEM, SMEM),
            scratch_shapes=[
                pltpu.VMEM((2, NAUX, NB2, NB2), jnp.bfloat16),
                square, square, square,
                pltpu.VMEM((2, NB2, NB2), jnp.bfloat16),
                square,
                pltpu.VMEM((2, NB, NB2), f32),
                pltpu.SemaphoreType.DMA((CHUNKS,)),
            ],
            compiler_params=params(40),
            name="scf",
        )(pos, pairs, probe_pos, mine, other, core_ham, probe_ints, ri_ints)
    partner = lax.ppermute(give, "inner", swap)
    got = []
    for k in range(1, N_Y):
        step = [(i, (i + 2 * k) % n_inner) for i in range(n_inner)]
        got.append(lax.ppermute(jnp.stack([keep[k], partner[k]]), "inner", step))

    with jax.named_scope("route"):
        slots = pl.pallas_call(
            route_kernel,
            out_shape=jax.ShapeDtypeStruct((N_GROUP, CAP // 2, 8, 128), f32),
            in_specs=[SMEM, SMEM] + [VMEM] * 5,
            out_specs=VMEM,
            scratch_shapes=[pltpu.SMEM((N_GROUP,), i32), pltpu.SMEM((2 * DIM_GRP,), i32),
                            pltpu.SMEM((2 * DIM_GRP,), i32)],
            name="route",
        )(pos, pairs, keep[0], partner[0], *got)
    homed = lax.all_to_all(slots, "group", split_axis=0, concat_axis=0, tiled=True)

    with jax.named_scope("home"):
        frag_weight = pl.pallas_call(
            home_kernel,
            out_shape=jax.ShapeDtypeStruct((FRAG_GRP, 8, NB), f32),
            in_specs=[SMEM, VMEM],
            out_specs=VMEM,
            name="home",
        )(table, homed)
    return (frag_weight, energy)


def solution(mesh):
    in_specs = (
        P("group", None, None),
        P("group", None),
        P(None, "group"),
        P(),
        P(None, ("group", "inner")),
        P(("group", "inner"), None, None),
        P(("group", "inner"), None, None, None),
        P(("group", "inner"), None, None, None),
    )
    out_specs = (P("group", "inner", None), P(("group", "inner")))
    return jax.shard_map(
        per_device, mesh=mesh, in_specs=in_specs, out_specs=out_specs, check_vma=False
    )
```

```python
import jax
import jax.numpy as jnp
from jax import lax
from jax.experimental import pallas as pl
from jax.experimental.pallas import tpu as pltpu
from jax.sharding import PartitionSpec as P

NB = 64
NB2 = 128
NAUX = 256
ATOMS = 16
NPROBE = 8
ITERS = 3
FRAG_GRP = 64
DIM_GRP = 16
CAP = 4
N_GROUP = 16
N_INNER = 8
SITE_ROWS = 8
HALF = SITE_ROWS // 2
ROWS = NB + 4 * HALF

STEP = 128
PART = 4
CHUNKS = 4

damping = 0.1
highest = lax.Precision.HIGHEST
VMEM = pl.BlockSpec(memory_space=pltpu.VMEM)
SMEM = pl.BlockSpec(memory_space=pltpu.SMEM)
ANY = pl.BlockSpec(memory_space=pl.ANY)


def dot32(a, b):
    return jnp.dot(a, b, precision=highest, preferred_element_type=jnp.float32)


def iota(shape, dim):
    return lax.broadcasted_iota(jnp.int32, shape, dim)


def owner_of(frag):
    return lax.shift_right_logical(frag, 6)


def place():
    inner = lax.axis_index("inner")
    return lax.axis_index("group"), inner // 2, inner % 2


def pack_kernel(pairs, dens_hbm, ref_charge, site_pos, send, table, dens, found, sem, found_sem):
    group, _, core = place()
    load = pltpu.make_async_copy(dens_hbm, dens, sem)
    load.start()

    frags = pairs[...]
    mine = (owner_of(frags) == group).astype(jnp.float32)
    columns = pairs.shape[1]
    pad = jnp.zeros((14, columns), jnp.float32)
    hits = jnp.concatenate([mine, pad], axis=0).astype(jnp.bfloat16)
    rows, cols = iota((columns, columns), 0), iota((columns, columns), 1)
    together = rows // DIM_GRP == cols // DIM_GRP
    ahead = jnp.logical_and(together, rows < cols).astype(jnp.bfloat16)
    before = jnp.dot(hits, ahead, preferred_element_type=jnp.float32)
    in_all = jnp.dot(hits, together.astype(jnp.bfloat16), preferred_element_type=jnp.float32)
    rank = jnp.concatenate([before[0:1], before[1:2] + in_all[0:1]], axis=0)
    local = lax.bitwise_and(frags, FRAG_GRP - 1).astype(jnp.float32)
    entries = []
    for s in range(CAP):
        taken = jnp.where(rank == s, mine * local, 0.0)
        entries.append(taken[0:1] + taken[1:2])
    entries.append(mine[0:1] + mine[1:2])
    entries = jnp.concatenate(entries + [pad[:16 - len(entries)]], axis=0).astype(jnp.bfloat16)
    segment = (iota((columns, 128), 0) // DIM_GRP == iota((columns, 128), 1)).astype(jnp.bfloat16)
    entries = jnp.dot(entries, segment, preferred_element_type=jnp.float32)[:8].astype(jnp.int32)
    table[...] = entries
    tell = pltpu.make_async_copy(table, found, found_sem)
    tell.start()
    load.wait()

    blocks = dens[...].reshape(FRAG_GRP, NB // 8, 8, NB)
    lane = iota((FRAG_GRP, 8, NB), 2)
    diagonal = blocks[:, 0]
    for i in range(1, NB // 8):
        diagonal = jnp.where(lane // 8 == i, blocks[:, i], diagonal)
    diagonal = jnp.sum(jnp.where(lane % 8 == iota((FRAG_GRP, 8, NB), 1), diagonal, 0.0), axis=1)
    spread = (iota((NB, 128), 0) // (NB // ATOMS) == iota((NB, 128), 1) % ATOMS).astype(jnp.float32)
    repeat = (iota((ATOMS, 128), 0) == iota((ATOMS, 128), 1) % ATOMS).astype(jnp.float32)
    given = lax.dot_general(ref_charge[...], repeat, (((0,), (0,)), ((), ())),
                            precision=highest, preferred_element_type=jnp.float32)
    charge = given - dot32(diagonal, spread)
    here = iota((FRAG_GRP, 128), 0) % (128 // ATOMS) == iota((FRAG_GRP, 128), 1) // ATOMS
    charge = jnp.sum(jnp.where(here, charge, 0.0).reshape(SITE_ROWS, 128 // ATOMS, 128), axis=1)

    sites = []
    for c in range(3):
        for r in range(HALF):
            low = site_pos[c:c + 1, r * 128:(r + 1) * 128]
            high = site_pos[c:c + 1, (r + HALF) * 128:(r + HALF + 1) * 128]
            sites.append(jnp.where(core == 0, low, high))
    sites = jnp.concatenate(sites + [jnp.where(core == 0, charge[:HALF], charge[HALF:])], axis=0)

    tell.wait()
    for g in range(N_GROUP):
        pair = [dens[found[2 * core + s, g]] for s in range(2)]
        send[g, :NB] = jnp.concatenate(pair, axis=1)
        send[g, NB:] = sites


def scf_kernel(pairs, pairs_wide, probe_pos, mine, other, core_any, probes_any, ri_hbm,
               blocks, energy, ri, start, fixed, dens, packed, fock, weighted, frags, sites,
               core_ham, probe_ints, ri_sems, frag_sems, late_sems):
    group, chip, core = place()
    per_chunk = NAUX // CHUNKS

    def load(c, d):
        part = pl.ds(c * per_chunk, per_chunk)
        return pltpu.make_async_copy(ri_hbm.at[d, part], ri.at[d, part], ri_sems.at[c, d])

    def load_chunk(c):
        load(c, 0).start()
        load(c, 1).start()

    load_chunk(0)
    first_dimer = (2 * chip + core) * 2
    left = iota((NB, NB2), 1) < NB

    owners = owner_of(pairs_wide[...])
    column = iota(owners.shape, 1)
    in_group = column // DIM_GRP == group
    first_row = iota(owners.shape, 0) == 0

    def load_fragment(i):
        side = i % 2
        at = group * DIM_GRP + first_dimer + i // 2
        owner = owner_of(pairs[side, at])
        if side == 0:
            earlier = jnp.logical_and(first_row, column < at)
        else:
            earlier = jnp.logical_or(first_row, column < at)
        hit = jnp.logical_and(jnp.logical_and(owners == owner, in_group), earlier)
        rank = jnp.sum(hit.astype(jnp.int32))

        @pl.when(rank // 2 == core)
        def _():
            pltpu.make_async_copy(mine.at[owner, pl.ds(0, NB)], frags.at[i], frag_sems.at[i]).start()

        @pl.when(rank // 2 != core)
        def _():
            pltpu.make_async_copy(other.at[owner, pl.ds(0, NB)], frags.at[i], frag_sems.at[i]).start()

        return rank

    ranks = [load_fragment(i) for i in range(4)]
    late = [pltpu.make_async_copy(mine.at[:, pl.ds(NB, ROWS - NB)], sites.at[0], late_sems.at[0]),
            pltpu.make_async_copy(other.at[:, pl.ds(NB, ROWS - NB)], sites.at[1], late_sems.at[1]),
            pltpu.make_async_copy(core_any, core_ham, late_sems.at[2]),
            pltpu.make_async_copy(probes_any, probe_ints, late_sems.at[3])]

    for d in range(2):
        halves = []
        for side in range(2):
            i = 2 * d + side
            pltpu.make_async_copy(mine.at[0, pl.ds(0, NB)], frags.at[i], frag_sems.at[i]).wait()
            rows = frags[i]
            halves.append(jnp.where(ranks[i] % 2 == side, rows, pltpu.roll(rows, NB, 1)))
        start[d, :NB] = jnp.where(left, halves[0], 0.0)
        start[d, NB:] = jnp.where(left, 0.0, halves[1])
        dens[d] = start[d]

    def fill_fixed():
        def gathered(c):
            rows = slice(HALF * c, HALF * (c + 1))
            return jnp.concatenate([sites[0, :, rows], sites[1, :, rows]], axis=1)

        xs, ys, zs, charge = (gathered(c) for c in range(4))
        shape = (N_GROUP, SITE_ROWS, 128)
        row = iota(shape, 1)
        row = jnp.where(row < HALF, row + HALF * core, row - HALF * core)
        site_frag = iota(shape, 0) * FRAG_GRP + row * (128 // ATOMS) + iota(shape, 2) // ATOMS
        for d in range(2):
            at = group * DIM_GRP + first_dimer + d
            keep_site = jnp.logical_and(site_frag != pairs[0, at], site_frag != pairs[1, at])
            kept = jnp.where(keep_site, charge, 0.0)
            total = core_ham[d]
            for k in range(NPROBE):
                p = d * NPROBE + k
                dx, dy, dz = xs - probe_pos[0, p], ys - probe_pos[1, p], zs - probe_pos[2, p]
                terms = kept * lax.rsqrt(dx * dx + dy * dy + dz * dz + 1.0)
                weight = jnp.sum(jnp.sum(terms, axis=0), axis=(0, 1), keepdims=True)
                total = total + weight * probe_ints[d, k].astype(jnp.float32)
            fixed[d] = total

    eye = iota((NB2, NB2), 0) == iota((NB2, NB2), 1)
    zero = jnp.zeros((NB2, NB2), jnp.bfloat16)

    def accumulate(first, count):
        both = jnp.concatenate([jnp.concatenate([packed[0], zero], axis=1),
                                jnp.concatenate([zero, packed[1]], axis=1)], axis=0)
        sums = [fock[0], fock[1]]
        for g in range(count // PART):
            at = pl.ds(first + g * PART, PART)
            parts = [ri[d, at] for d in range(2)]
            wide = jnp.concatenate([p.reshape(PART * NB2, NB2) for p in parts], axis=1)
            half = jnp.dot(wide, both, preferred_element_type=jnp.float32)
            rows = []
            for d in range(2):
                squares = []
                for i in range(PART):
                    square = half[i * NB2:(i + 1) * NB2, d * NB2:(d + 1) * NB2]
                    fit = (parts[d][i] * packed[d]).astype(jnp.float32).reshape(-1, 8, NB2)
                    fit = jnp.sum(jnp.sum(fit, axis=0), axis=0, keepdims=True)
                    fit = jnp.sum(fit, axis=1, keepdims=True)
                    fit = -2.0 * fit.astype(jnp.bfloat16).astype(jnp.float32)
                    squares.append(jnp.where(eye, square + fit, square).astype(jnp.bfloat16))
                rows.append(jnp.concatenate(squares, axis=1))
            out = jnp.dot(jnp.concatenate(rows, axis=0), wide, preferred_element_type=jnp.float32)
            sums[0] = sums[0] + out[:NB2, :NB2]
            sums[1] = sums[1] + out[NB2:, NB2:]
        fock[0] = sums[0]
        fock[1] = sums[1]

    def begin():
        packed[...] = dens[...].astype(jnp.bfloat16)
        fock[...] = jnp.zeros_like(fock)

    def update():
        for d in range(2):
            matrix = fixed[d] - 0.5 * fock[d]
            fock[d] = matrix
            dens[d] = start[d] - damping * dot32(dot32(start[d], matrix), start[d])

    begin()

    def arriving(c, carry):
        load(c, 0).wait()
        load(c, 1).wait()

        @pl.when(c + 1 < CHUNKS)
        def _():
            load_chunk(c + 1)

        @pl.when(c == CHUNKS - 1)
        def _():
            for copy in late:
                copy.start()

        accumulate(c * per_chunk, per_chunk)
        return carry

    lax.fori_loop(0, CHUNKS, arriving, 0)
    for copy in late:
        copy.wait()
    fill_fixed()
    update()

    def sweep(t, carry):
        begin()

        def body(step, inner_carry):
            accumulate(step * STEP, STEP)
            return inner_carry

        lax.fori_loop(0, NAUX // STEP, body, 0)
        update()
        return carry

    lax.fori_loop(1, ITERS, sweep, 0)

    for d in range(2):
        matrix, density = fock[d], dens[d]
        energy[d] = (0.5 / NB2) * jnp.sum(density * (core_ham[d] + matrix))
        block = dot32(dot32(density, matrix), density)
        weighted[d] = jnp.where(left, block[:NB], block[NB:])
    for j in range(N_INNER):
        for d in range(2):
            blocks[j, d] = weighted[d, j * 8:(j + 1) * 8]


def route_kernel(pairs, got, out, count, owners, ranks):
    group = lax.axis_index("group")
    for o in range(N_GROUP):
        count[o] = 0
    for side in range(2):
        for dimer in range(DIM_GRP):
            owner = owner_of(pairs[side, group * DIM_GRP + dimer])
            rank = count[owner]
            owners[2 * dimer + side] = owner
            ranks[2 * dimer + side] = rank
            count[owner] = rank + 1
    out[...] = jnp.zeros_like(out)
    lane_half = iota((8, 128), 1) // NB
    for dimer in range(DIM_GRP):
        block = got[dimer // 2, dimer % 2]
        turned = pltpu.roll(block, NB, 1)
        for side in range(2):
            owner, rank = owners[2 * dimer + side], ranks[2 * dimer + side]
            half = lax.rem(rank, 2)
            value = jnp.where(half == side, block, turned)
            here = (owner, lax.div(rank, 2))
            out[here] = jnp.where(lane_half == half, value, out[here])


def home_kernel(table, got, out):
    out[...] = jnp.zeros_like(out)
    for g in range(N_GROUP):
        for s in range(CAP):
            at = table[s, g]
            block = got[g, s // 2]
            value = block[:, :NB] if s % 2 == 0 else pltpu.roll(block, NB, 1)[:, :NB]
            out[at] = out[at] + jnp.where(s < table[CAP, g], value, 0.0)


def params(mib):
    return pltpu.CompilerParams(vmem_limit_bytes=mib * 1024 * 1024)


def per_device(densities, ref_charge, site_pos, dimer_pairs, probe_pos, core_ham, probe_ints, ri_ints):
    f32, i32 = jnp.float32, jnp.int32
    pairs = dimer_pairs.T
    swap = [(i, i ^ 1) for i in range(N_INNER)]

    with jax.named_scope("pack"):
        send, table = pl.pallas_call(
            pack_kernel,
            out_shape=(jax.ShapeDtypeStruct((N_GROUP, ROWS, 128), f32),
                       jax.ShapeDtypeStruct((8, 128), i32)),
            in_specs=[VMEM, ANY, VMEM, VMEM],
            out_specs=(VMEM, VMEM),
            scratch_shapes=[pltpu.VMEM((FRAG_GRP, NB, NB), f32), pltpu.SMEM((8, 128), i32),
                            pltpu.SemaphoreType.DMA, pltpu.SemaphoreType.DMA],
            compiler_params=params(58),
            name="pack",
        )(pairs, densities, ref_charge.T, site_pos)
    mine = lax.all_to_all(send, "group", split_axis=0, concat_axis=0, tiled=True)
    other = lax.ppermute(mine, "inner", swap)

    with jax.named_scope("scf"):
        square = pltpu.VMEM((2, NB2, NB2), f32)
        blocks, energy = pl.pallas_call(
            scf_kernel,
            out_shape=(jax.ShapeDtypeStruct((N_INNER, 2, 8, 128), f32), jax.ShapeDtypeStruct((2,), f32)),
            in_specs=[SMEM, VMEM, SMEM, ANY, ANY, ANY, ANY, ANY],
            out_specs=(VMEM, SMEM),
            scratch_shapes=[
                pltpu.VMEM((2, NAUX, NB2, NB2), jnp.bfloat16),
                square, square, square,
                pltpu.VMEM((2, NB2, NB2), jnp.bfloat16),
                square,
                pltpu.VMEM((2, NB, NB2), f32),
                pltpu.VMEM((4, NB, 128), f32),
                pltpu.VMEM((2, N_GROUP, ROWS - NB, 128), f32),
                square,
                pltpu.VMEM((2, NPROBE, NB2, NB2), jnp.bfloat16),
                pltpu.SemaphoreType.DMA((CHUNKS, 2)),
                pltpu.SemaphoreType.DMA((4,)),
                pltpu.SemaphoreType.DMA((4,)),
            ],
            compiler_params=params(58),
            name="scf",
        )(pairs, pairs, probe_pos, mine, other, core_ham, probe_ints, ri_ints)
    rows = lax.all_to_all(blocks, "inner", split_axis=0, concat_axis=0, tiled=True)

    with jax.named_scope("route"):
        slots = pl.pallas_call(
            route_kernel,
            out_shape=jax.ShapeDtypeStruct((N_GROUP, CAP // 2, 8, 128), f32),
            in_specs=[SMEM, VMEM],
            out_specs=VMEM,
            scratch_shapes=[pltpu.SMEM((N_GROUP,), i32), pltpu.SMEM((2 * DIM_GRP,), i32),
                            pltpu.SMEM((2 * DIM_GRP,), i32)],
            name="route",
        )(pairs, rows)
    homed = lax.all_to_all(slots, "group", split_axis=0, concat_axis=0, tiled=True)

    with jax.named_scope("home"):
        frag_weight = pl.pallas_call(
            home_kernel,
            out_shape=jax.ShapeDtypeStruct((FRAG_GRP, 8, NB), f32),
            in_specs=[SMEM, VMEM],
            out_specs=VMEM,
            name="home",
        )(table, homed)
    return (frag_weight, energy)


def solution(mesh):
    in_specs = (
        P("group", None, None),
        P("group", None),
        P(None, "group"),
        P(),
        P(None, ("group", "inner")),
        P(("group", "inner"), None, None),
        P(("group", "inner"), None, None, None),
        P(("group", "inner"), None, None, None),
    )
    out_specs = (P("group", "inner", None), P(("group", "inner")))
    return jax.shard_map(
        per_device, mesh=mesh, in_specs=in_specs, out_specs=out_specs, check_vma=False
    )
```

```python
import jax
import jax.numpy as jnp
from jax import lax
from jax.experimental import pallas as pl
from jax.experimental.pallas import tpu as pltpu
from jax.sharding import PartitionSpec as P

NB = 64
NB2 = 128
NAUX = 256
ATOMS = 16
NPROBE = 8
ITERS = 3
FRAG_GRP = 64
DIM_GRP = 16
CAP = 4
N_GROUP = 16
N_INNER = 8
SITE_ROWS = 8
HALF = SITE_ROWS // 2
TRI = NB - NB // 4
ROWS = TRI + 4 * HALF

STEP = 128
PART = 4
CHUNKS = 4

damping = 0.1
highest = lax.Precision.HIGHEST
VMEM = pl.BlockSpec(memory_space=pltpu.VMEM)
SMEM = pl.BlockSpec(memory_space=pltpu.SMEM)
ANY = pl.BlockSpec(memory_space=pl.ANY)


def dot32(a, b):
    return jnp.dot(a, b, precision=highest, preferred_element_type=jnp.float32)


def iota(shape, dim):
    return lax.broadcasted_iota(jnp.int32, shape, dim)


def owner_of(frag):
    return lax.shift_right_logical(frag, 6)


def place():
    inner = lax.axis_index("inner")
    return lax.axis_index("group"), inner // 2, inner % 2


def pack_kernel(pairs, dens_hbm, ref_charge, site_pos, send, table, dens, found, sem, found_sem):
    group, _, core = place()
    load = pltpu.make_async_copy(dens_hbm, dens, sem)
    load.start()

    frags = pairs[...]
    mine = (owner_of(frags) == group).astype(jnp.float32)
    columns = pairs.shape[1]
    pad = jnp.zeros((14, columns), jnp.float32)
    hits = jnp.concatenate([mine, pad], axis=0).astype(jnp.bfloat16)
    rows, cols = iota((columns, columns), 0), iota((columns, columns), 1)
    together = rows // DIM_GRP == cols // DIM_GRP
    ahead = jnp.logical_and(together, rows < cols).astype(jnp.bfloat16)
    before = jnp.dot(hits, ahead, preferred_element_type=jnp.float32)
    in_all = jnp.dot(hits, together.astype(jnp.bfloat16), preferred_element_type=jnp.float32)
    rank = jnp.concatenate([before[0:1], before[1:2] + in_all[0:1]], axis=0)
    local = lax.bitwise_and(frags, FRAG_GRP - 1).astype(jnp.float32)
    entries = []
    for s in range(CAP):
        taken = jnp.where(rank == s, mine * local, 0.0)
        entries.append(taken[0:1] + taken[1:2])
    entries.append(mine[0:1] + mine[1:2])
    entries = jnp.concatenate(entries + [pad[:16 - len(entries)]], axis=0).astype(jnp.bfloat16)
    segment = (iota((columns, 128), 0) // DIM_GRP == iota((columns, 128), 1)).astype(jnp.bfloat16)
    entries = jnp.dot(entries, segment, preferred_element_type=jnp.float32)[:8].astype(jnp.int32)
    table[...] = entries
    tell = pltpu.make_async_copy(table, found, found_sem)
    tell.start()
    load.wait()

    blocks = dens[...].reshape(FRAG_GRP, NB // 8, 8, NB)
    lane = iota((FRAG_GRP, 8, NB), 2)
    diagonal = blocks[:, 0]
    for i in range(1, NB // 8):
        diagonal = jnp.where(lane // 8 == i, blocks[:, i], diagonal)
    diagonal = jnp.sum(jnp.where(lane % 8 == iota((FRAG_GRP, 8, NB), 1), diagonal, 0.0), axis=1)
    spread = (iota((NB, 128), 0) // (NB // ATOMS) == iota((NB, 128), 1) % ATOMS).astype(jnp.float32)
    repeat = (iota((ATOMS, 128), 0) == iota((ATOMS, 128), 1) % ATOMS).astype(jnp.float32)
    given = lax.dot_general(ref_charge[...], repeat, (((0,), (0,)), ((), ())),
                            precision=highest, preferred_element_type=jnp.float32)
    charge = given - dot32(diagonal, spread)
    here = iota((FRAG_GRP, 128), 0) % (128 // ATOMS) == iota((FRAG_GRP, 128), 1) // ATOMS
    charge = jnp.sum(jnp.where(here, charge, 0.0).reshape(SITE_ROWS, 128 // ATOMS, 128), axis=1)

    sites = []
    for c in range(3):
        for r in range(HALF):
            low = site_pos[c:c + 1, r * 128:(r + 1) * 128]
            high = site_pos[c:c + 1, (r + HALF) * 128:(r + HALF + 1) * 128]
            sites.append(jnp.where(core == 0, low, high))
    sites = jnp.concatenate(sites + [jnp.where(core == 0, charge[:HALF], charge[HALF:])], axis=0)

    tell.wait()
    inner_half = iota((NB // 4, 128), 1) % NB < NB // 2
    for g in range(N_GROUP):
        pair = jnp.concatenate([dens[found[2 * core + s, g]] for s in range(2)], axis=1)
        send[g, :NB // 2] = pair[:NB // 2]
        send[g, NB // 2:TRI] = jnp.where(inner_half, pltpu.roll(pair[TRI:], 128 - NB // 2, 1), pair[NB // 2:TRI])
        send[g, TRI:] = sites


def scf_kernel(pairs, pairs_wide, probe_pos, mine, other, core_any, probes_any, ri_hbm,
               blocks, energy, ri, start, fixed, dens, packed, fock, weighted, frags, sites,
               core_ham, probe_ints, ri_sems, frag_sems, late_sems):
    group, chip, core = place()
    per_chunk = NAUX // CHUNKS

    def load(c, d):
        part = pl.ds(c * per_chunk, per_chunk)
        return pltpu.make_async_copy(ri_hbm.at[d, part], ri.at[d, part], ri_sems.at[c, d])

    def load_chunk(c):
        load(c, 0).start()
        load(c, 1).start()

    load_chunk(0)
    first_dimer = (2 * chip + core) * 2
    left = iota((NB, NB2), 1) < NB

    owners = owner_of(pairs_wide[...])
    column = iota(owners.shape, 1)
    in_group = column // DIM_GRP == group
    first_row = iota(owners.shape, 0) == 0

    def load_fragment(i):
        side = i % 2
        at = group * DIM_GRP + first_dimer + i // 2
        owner = owner_of(pairs[side, at])
        if side == 0:
            earlier = jnp.logical_and(first_row, column < at)
        else:
            earlier = jnp.logical_or(first_row, column < at)
        hit = jnp.logical_and(jnp.logical_and(owners == owner, in_group), earlier)
        rank = jnp.sum(hit.astype(jnp.int32))

        @pl.when(rank // 2 == core)
        def _():
            pltpu.make_async_copy(mine.at[owner, pl.ds(0, TRI)], frags.at[i], frag_sems.at[i]).start()

        @pl.when(rank // 2 != core)
        def _():
            pltpu.make_async_copy(other.at[owner, pl.ds(0, TRI)], frags.at[i], frag_sems.at[i]).start()

        return rank

    ranks = [load_fragment(i) for i in range(4)]
    late = [pltpu.make_async_copy(mine.at[:, pl.ds(TRI, ROWS - TRI)], sites.at[0], late_sems.at[0]),
            pltpu.make_async_copy(other.at[:, pl.ds(TRI, ROWS - TRI)], sites.at[1], late_sems.at[1]),
            pltpu.make_async_copy(core_any, core_ham, late_sems.at[2]),
            pltpu.make_async_copy(probes_any, probe_ints, late_sems.at[3])]

    lane, line = iota((NB2, NB2), 1), iota((NB2, NB2), 0)
    mirrored = jnp.logical_and(line // (NB // 2) == lane // (NB // 2) + 1, line // NB == lane // NB)
    stored = jnp.logical_and(line // NB == lane // NB, jnp.logical_not(mirrored))
    for d in range(2):
        lines = []
        for side in range(2):
            i = 2 * d + side
            pltpu.make_async_copy(mine.at[0, pl.ds(0, TRI)], frags.at[i], frag_sems.at[i]).wait()
            rows = frags[i]
            rows = jnp.where(ranks[i] % 2 == side, rows, pltpu.roll(rows, NB, 1))
            lines += [rows, pltpu.roll(rows[NB // 2:], NB // 2, 1)]
        upper = jnp.where(stored, jnp.concatenate(lines, axis=0), 0.0)
        start[d] = jnp.where(mirrored, upper.T, upper)
        dens[d] = start[d]

    def fill_fixed():
        def gathered(c):
            rows = slice(HALF * c, HALF * (c + 1))
            return jnp.concatenate([sites[0, :, rows], sites[1, :, rows]], axis=1)

        xs, ys, zs, charge = (gathered(c) for c in range(4))
        shape = (N_GROUP, SITE_ROWS, 128)
        row = iota(shape, 1)
        row = jnp.where(row < HALF, row + HALF * core, row - HALF * core)
        site_frag = iota(shape, 0) * FRAG_GRP + row * (128 // ATOMS) + iota(shape, 2) // ATOMS
        for d in range(2):
            at = group * DIM_GRP + first_dimer + d
            keep_site = jnp.logical_and(site_frag != pairs[0, at], site_frag != pairs[1, at])
            kept = jnp.where(keep_site, charge, 0.0)
            total = core_ham[d]
            for k in range(NPROBE):
                p = d * NPROBE + k
                dx, dy, dz = xs - probe_pos[0, p], ys - probe_pos[1, p], zs - probe_pos[2, p]
                terms = kept * lax.rsqrt(dx * dx + dy * dy + dz * dz + 1.0)
                weight = jnp.sum(jnp.sum(terms, axis=0), axis=(0, 1), keepdims=True)
                total = total + weight * probe_ints[d, k].astype(jnp.float32)
            fixed[d] = total

    eye = iota((NB2, NB2), 0) == iota((NB2, NB2), 1)
    zero = jnp.zeros((NB2, NB2), jnp.bfloat16)

    def accumulate(first, count):
        both = jnp.concatenate([jnp.concatenate([packed[0], zero], axis=1),
                                jnp.concatenate([zero, packed[1]], axis=1)], axis=0)
        sums = [fock[0], fock[1]]
        for g in range(count // PART):
            at = pl.ds(first + g * PART, PART)
            parts = [ri[d, at] for d in range(2)]
            wide = jnp.concatenate([p.reshape(PART * NB2, NB2) for p in parts], axis=1)
            half = jnp.dot(wide, both, preferred_element_type=jnp.float32)
            rows = []
            for d in range(2):
                squares = []
                for i in range(PART):
                    square = half[i * NB2:(i + 1) * NB2, d * NB2:(d + 1) * NB2]
                    fit = (parts[d][i] * packed[d]).astype(jnp.float32).reshape(-1, 8, NB2)
                    fit = jnp.sum(jnp.sum(fit, axis=0), axis=0, keepdims=True)
                    fit = jnp.sum(fit, axis=1, keepdims=True)
                    fit = -2.0 * fit.astype(jnp.bfloat16).astype(jnp.float32)
                    squares.append(jnp.where(eye, square + fit, square).astype(jnp.bfloat16))
                rows.append(jnp.concatenate(squares, axis=1))
            out = jnp.dot(jnp.concatenate(rows, axis=0), wide, preferred_element_type=jnp.float32)
            sums[0] = sums[0] + out[:NB2, :NB2]
            sums[1] = sums[1] + out[NB2:, NB2:]
        fock[0] = sums[0]
        fock[1] = sums[1]

    def begin():
        packed[...] = dens[...].astype(jnp.bfloat16)
        fock[...] = jnp.zeros_like(fock)

    def update():
        for d in range(2):
            matrix = fixed[d] - 0.5 * fock[d]
            fock[d] = matrix
            dens[d] = start[d] - damping * dot32(dot32(start[d], matrix), start[d])

    begin()

    def arriving(c, carry):
        load(c, 0).wait()
        load(c, 1).wait()

        @pl.when(c + 1 < CHUNKS)
        def _():
            load_chunk(c + 1)

        @pl.when(c == CHUNKS - 1)
        def _():
            for copy in late:
                copy.start()

        accumulate(c * per_chunk, per_chunk)
        return carry

    lax.fori_loop(0, CHUNKS, arriving, 0)
    for copy in late:
        copy.wait()
    fill_fixed()
    update()

    def sweep(t, carry):
        begin()

        def body(step, inner_carry):
            accumulate(step * STEP, STEP)
            return inner_carry

        lax.fori_loop(0, NAUX // STEP, body, 0)
        update()
        return carry

    lax.fori_loop(1, ITERS, sweep, 0)

    for d in range(2):
        matrix, density = fock[d], dens[d]
        energy[d] = (0.5 / NB2) * jnp.sum(density * (core_ham[d] + matrix))
        block = dot32(dot32(density, matrix), density)
        weighted[d] = jnp.where(left, block[:NB], block[NB:])
    for j in range(N_INNER):
        for d in range(2):
            blocks[j, d] = weighted[d, j * 8:(j + 1) * 8]


def route_kernel(pairs, got, out, count, owners, ranks):
    group = lax.axis_index("group")
    for o in range(N_GROUP):
        count[o] = 0
    for side in range(2):
        for dimer in range(DIM_GRP):
            owner = owner_of(pairs[side, group * DIM_GRP + dimer])
            rank = count[owner]
            owners[2 * dimer + side] = owner
            ranks[2 * dimer + side] = rank
            count[owner] = rank + 1
    out[...] = jnp.zeros_like(out)
    lane_half = iota((8, 128), 1) // NB
    for dimer in range(DIM_GRP):
        block = got[dimer // 2, dimer % 2]
        turned = pltpu.roll(block, NB, 1)
        for side in range(2):
            owner, rank = owners[2 * dimer + side], ranks[2 * dimer + side]
            half = lax.rem(rank, 2)
            value = jnp.where(half == side, block, turned)
            here = (owner, lax.div(rank, 2))
            out[here] = jnp.where(lane_half == half, value, out[here])


def home_kernel(table, got, out):
    out[...] = jnp.zeros_like(out)
    for g in range(N_GROUP):
        for s in range(CAP):
            at = table[s, g]
            block = got[g, s // 2]
            value = block[:, :NB] if s % 2 == 0 else pltpu.roll(block, NB, 1)[:, :NB]
            out[at] = out[at] + jnp.where(s < table[CAP, g], value, 0.0)


def params(mib):
    return pltpu.CompilerParams(vmem_limit_bytes=mib * 1024 * 1024)


def per_device(densities, ref_charge, site_pos, dimer_pairs, probe_pos, core_ham, probe_ints, ri_ints):
    f32, i32 = jnp.float32, jnp.int32
    pairs = dimer_pairs.T
    swap = [(i, i ^ 1) for i in range(N_INNER)]

    with jax.named_scope("pack"):
        send, table = pl.pallas_call(
            pack_kernel,
            out_shape=(jax.ShapeDtypeStruct((N_GROUP, ROWS, 128), f32),
                       jax.ShapeDtypeStruct((8, 128), i32)),
            in_specs=[VMEM, ANY, VMEM, VMEM],
            out_specs=(VMEM, VMEM),
            scratch_shapes=[pltpu.VMEM((FRAG_GRP, NB, NB), f32), pltpu.SMEM((8, 128), i32),
                            pltpu.SemaphoreType.DMA, pltpu.SemaphoreType.DMA],
            compiler_params=params(58),
            name="pack",
        )(pairs, densities, ref_charge.T, site_pos)
    mine = lax.all_to_all(send, "group", split_axis=0, concat_axis=0, tiled=True)
    other = lax.ppermute(mine, "inner", swap)

    with jax.named_scope("scf"):
        square = pltpu.VMEM((2, NB2, NB2), f32)
        blocks, energy = pl.pallas_call(
            scf_kernel,
            out_shape=(jax.ShapeDtypeStruct((N_INNER, 2, 8, 128), f32), jax.ShapeDtypeStruct((2,), f32)),
            in_specs=[SMEM, VMEM, SMEM, ANY, ANY, ANY, ANY, ANY],
            out_specs=(VMEM, SMEM),
            scratch_shapes=[
                pltpu.VMEM((2, NAUX, NB2, NB2), jnp.bfloat16),
                square, square, square,
                pltpu.VMEM((2, NB2, NB2), jnp.bfloat16),
                square,
                pltpu.VMEM((2, NB, NB2), f32),
                pltpu.VMEM((4, TRI, 128), f32),
                pltpu.VMEM((2, N_GROUP, ROWS - TRI, 128), f32),
                square,
                pltpu.VMEM((2, NPROBE, NB2, NB2), jnp.bfloat16),
                pltpu.SemaphoreType.DMA((CHUNKS, 2)),
                pltpu.SemaphoreType.DMA((4,)),
                pltpu.SemaphoreType.DMA((4,)),
            ],
            compiler_params=params(58),
            name="scf",
        )(pairs, pairs, probe_pos, mine, other, core_ham, probe_ints, ri_ints)
    rows = lax.all_to_all(blocks, "inner", split_axis=0, concat_axis=0, tiled=True)

    with jax.named_scope("route"):
        slots = pl.pallas_call(
            route_kernel,
            out_shape=jax.ShapeDtypeStruct((N_GROUP, CAP // 2, 8, 128), f32),
            in_specs=[SMEM, VMEM],
            out_specs=VMEM,
            scratch_shapes=[pltpu.SMEM((N_GROUP,), i32), pltpu.SMEM((2 * DIM_GRP,), i32),
                            pltpu.SMEM((2 * DIM_GRP,), i32)],
            name="route",
        )(pairs, rows)
    homed = lax.all_to_all(slots, "group", split_axis=0, concat_axis=0, tiled=True)

    with jax.named_scope("home"):
        frag_weight = pl.pallas_call(
            home_kernel,
            out_shape=jax.ShapeDtypeStruct((FRAG_GRP, 8, NB), f32),
            in_specs=[SMEM, VMEM],
            out_specs=VMEM,
            name="home",
        )(table, homed)
    return (frag_weight, energy)


def solution(mesh):
    in_specs = (
        P("group", None, None),
        P("group", None),
        P(None, "group"),
        P(),
        P(None, ("group", "inner")),
        P(("group", "inner"), None, None),
        P(("group", "inner"), None, None, None),
        P(("group", "inner"), None, None, None),
    )
    out_specs = (P("group", "inner", None), P(("group", "inner")))
    return jax.shard_map(
        per_device, mesh=mesh, in_specs=in_specs, out_specs=out_specs, check_vma=False
    )
```

```python
import jax
import jax.numpy as jnp
from jax import lax
from jax.experimental import pallas as pl
from jax.experimental.pallas import tpu as pltpu
from jax.sharding import PartitionSpec as P

NB = 64
NB2 = 128
NAUX = 256
ATOMS = 16
NPROBE = 8
ITERS = 3
FRAG_GRP = 64
DIM_GRP = 16
CAP = 4
N_GROUP = 16
N_INNER = 8
SITE_ROWS = 8
HALF = SITE_ROWS // 2
TRI = NB // 2 + 8
ROWS = TRI + 4 * HALF

STEP = 128
PART = 4
CHUNKS = 4

damping = 0.1
highest = lax.Precision.HIGHEST
VMEM = pl.BlockSpec(memory_space=pltpu.VMEM)
SMEM = pl.BlockSpec(memory_space=pltpu.SMEM)
ANY = pl.BlockSpec(memory_space=pl.ANY)


def dot32(a, b):
    return jnp.dot(a, b, precision=highest, preferred_element_type=jnp.float32)


def iota(shape, dim):
    return lax.broadcasted_iota(jnp.int32, shape, dim)


def owner_of(frag):
    return lax.shift_right_logical(frag, 6)


def place():
    inner = lax.axis_index("inner")
    return lax.axis_index("group"), inner // 2, inner % 2


def pack_kernel(pairs, dens_hbm, ref_charge, site_pos, send, table, dens, found, sem, found_sem):
    group, _, core = place()
    load = pltpu.make_async_copy(dens_hbm, dens, sem)
    load.start()

    frags = pairs[...]
    mine = (owner_of(frags) == group).astype(jnp.float32)
    columns = pairs.shape[1]
    pad = jnp.zeros((14, columns), jnp.float32)
    hits = jnp.concatenate([mine, pad], axis=0).astype(jnp.bfloat16)
    rows, cols = iota((columns, columns), 0), iota((columns, columns), 1)
    together = rows // DIM_GRP == cols // DIM_GRP
    ahead = jnp.logical_and(together, rows < cols).astype(jnp.bfloat16)
    before = jnp.dot(hits, ahead, preferred_element_type=jnp.float32)
    in_all = jnp.dot(hits, together.astype(jnp.bfloat16), preferred_element_type=jnp.float32)
    rank = jnp.concatenate([before[0:1], before[1:2] + in_all[0:1]], axis=0)
    local = lax.bitwise_and(frags, FRAG_GRP - 1).astype(jnp.float32)
    entries = []
    for s in range(CAP):
        taken = jnp.where(rank == s, mine * local, 0.0)
        entries.append(taken[0:1] + taken[1:2])
    entries.append(mine[0:1] + mine[1:2])
    entries = jnp.concatenate(entries + [pad[:16 - len(entries)]], axis=0).astype(jnp.bfloat16)
    segment = (iota((columns, 128), 0) // DIM_GRP == iota((columns, 128), 1)).astype(jnp.bfloat16)
    entries = jnp.dot(entries, segment, preferred_element_type=jnp.float32)[:8].astype(jnp.int32)
    table[...] = entries
    tell = pltpu.make_async_copy(table, found, found_sem)
    tell.start()
    load.wait()

    blocks = dens[...].reshape(FRAG_GRP, NB // 8, 8, NB)
    lane = iota((FRAG_GRP, 8, NB), 2)
    diagonal = blocks[:, 0]
    for i in range(1, NB // 8):
        diagonal = jnp.where(lane // 8 == i, blocks[:, i], diagonal)
    diagonal = jnp.sum(jnp.where(lane % 8 == iota((FRAG_GRP, 8, NB), 1), diagonal, 0.0), axis=1)
    spread = (iota((NB, 128), 0) // (NB // ATOMS) == iota((NB, 128), 1) % ATOMS).astype(jnp.float32)
    repeat = (iota((ATOMS, 128), 0) == iota((ATOMS, 128), 1) % ATOMS).astype(jnp.float32)
    given = lax.dot_general(ref_charge[...], repeat, (((0,), (0,)), ((), ())),
                            precision=highest, preferred_element_type=jnp.float32)
    charge = given - dot32(diagonal, spread)
    here = iota((FRAG_GRP, 128), 0) % (128 // ATOMS) == iota((FRAG_GRP, 128), 1) // ATOMS
    charge = jnp.sum(jnp.where(here, charge, 0.0).reshape(SITE_ROWS, 128 // ATOMS, 128), axis=1)

    sites = []
    for c in range(3):
        for r in range(HALF):
            low = site_pos[c:c + 1, r * 128:(r + 1) * 128]
            high = site_pos[c:c + 1, (r + HALF) * 128:(r + HALF + 1) * 128]
            sites.append(jnp.where(core == 0, low, high))
    sites = jnp.concatenate(sites + [jnp.where(core == 0, charge[:HALF], charge[HALF:])], axis=0)

    tell.wait()
    line, lane = iota((NB // 2, 128), 0), iota((NB // 2, 128), 1) % NB
    spare = line > lane
    on_diagonal = line == lane - NB // 2
    for g in range(N_GROUP):
        pair = jnp.concatenate([dens[found[2 * core + s, g]] for s in range(2)], axis=1)
        lower = pair[NB // 2:]
        send[g, :NB // 2] = jnp.where(spare, pltpu.roll(lower, 128 - NB // 2, 1), pair[:NB // 2])
        send[g, NB // 2:TRI] = jnp.sum(jnp.where(on_diagonal, lower, 0.0).reshape(-1, 8, 128), axis=0)
        send[g, TRI:] = sites


def scf_kernel(pairs, pairs_wide, probe_pos, mine, other, core_any, probes_any, ri_hbm,
               blocks, energy, ri, start, fixed, dens, packed, fock, weighted, frags, sites,
               core_ham, probe_ints, ri_sems, frag_sems, late_sems):
    group, chip, core = place()
    per_chunk = NAUX // CHUNKS

    def load(c, d):
        part = pl.ds(c * per_chunk, per_chunk)
        return pltpu.make_async_copy(ri_hbm.at[d, part], ri.at[d, part], ri_sems.at[c, d])

    def load_chunk(c):
        load(c, 0).start()
        load(c, 1).start()

    load_chunk(0)
    first_dimer = (2 * chip + core) * 2
    left = iota((NB, NB2), 1) < NB

    owners = owner_of(pairs_wide[...])
    column = iota(owners.shape, 1)
    in_group = column // DIM_GRP == group
    first_row = iota(owners.shape, 0) == 0

    def load_fragment(i):
        side = i % 2
        at = group * DIM_GRP + first_dimer + i // 2
        owner = owner_of(pairs[side, at])
        if side == 0:
            earlier = jnp.logical_and(first_row, column < at)
        else:
            earlier = jnp.logical_or(first_row, column < at)
        hit = jnp.logical_and(jnp.logical_and(owners == owner, in_group), earlier)
        rank = jnp.sum(hit.astype(jnp.int32))

        @pl.when(rank // 2 == core)
        def _():
            pltpu.make_async_copy(mine.at[owner, pl.ds(0, TRI)], frags.at[i], frag_sems.at[i]).start()

        @pl.when(rank // 2 != core)
        def _():
            pltpu.make_async_copy(other.at[owner, pl.ds(0, TRI)], frags.at[i], frag_sems.at[i]).start()

        return rank

    ranks = [load_fragment(i) for i in range(4)]
    late = [pltpu.make_async_copy(mine.at[:, pl.ds(TRI, ROWS - TRI)], sites.at[0], late_sems.at[0]),
            pltpu.make_async_copy(other.at[:, pl.ds(TRI, ROWS - TRI)], sites.at[1], late_sems.at[1]),
            pltpu.make_async_copy(core_any, core_ham, late_sems.at[2]),
            pltpu.make_async_copy(probes_any, probe_ints, late_sems.at[3])]

    lane, line = iota((NB2, NB2), 1), iota((NB2, NB2), 0)
    same = line // NB == lane // NB
    top, left_half = line % NB < NB // 2, lane % NB < NB // 2
    stored = jnp.logical_or(jnp.logical_and(top, jnp.logical_or(line <= lane, jnp.logical_not(left_half))),
                            jnp.logical_and(jnp.logical_not(left_half), line >= lane))
    low_diagonal = iota((NB // 2, NB2), 0) + NB // 2 == iota((NB // 2, NB2), 1) % NB
    for d in range(2):
        lines = []
        for side in range(2):
            i = 2 * d + side
            pltpu.make_async_copy(mine.at[0, pl.ds(0, TRI)], frags.at[i], frag_sems.at[i]).wait()
            rows = frags[i]
            rows = jnp.where(ranks[i] % 2 == side, rows, pltpu.roll(rows, NB, 1))
            upper = rows[:NB // 2]
            low = jnp.concatenate([rows[NB // 2:]] * (NB // 16), axis=0)
            lines += [upper, jnp.where(low_diagonal, low, pltpu.roll(upper, NB // 2, 1))]
        packed_once = jnp.concatenate(lines, axis=0)
        start[d] = jnp.where(same, jnp.where(stored, packed_once, packed_once.T), 0.0)
        dens[d] = start[d]

    def fill_fixed():
        def gathered(c):
            rows = slice(HALF * c, HALF * (c + 1))
            return jnp.concatenate([sites[0, :, rows], sites[1, :, rows]], axis=1)

        xs, ys, zs, charge = (gathered(c) for c in range(4))
        shape = (N_GROUP, SITE_ROWS, 128)
        row = iota(shape, 1)
        row = jnp.where(row < HALF, row + HALF * core, row - HALF * core)
        site_frag = iota(shape, 0) * FRAG_GRP + row * (128 // ATOMS) + iota(shape, 2) // ATOMS
        for d in range(2):
            at = group * DIM_GRP + first_dimer + d
            keep_site = jnp.logical_and(site_frag != pairs[0, at], site_frag != pairs[1, at])
            kept = jnp.where(keep_site, charge, 0.0)
            total = core_ham[d]
            for k in range(NPROBE):
                p = d * NPROBE + k
                dx, dy, dz = xs - probe_pos[0, p], ys - probe_pos[1, p], zs - probe_pos[2, p]
                terms = kept * lax.rsqrt(dx * dx + dy * dy + dz * dz + 1.0)
                weight = jnp.sum(jnp.sum(terms, axis=0), axis=(0, 1), keepdims=True)
                total = total + weight * probe_ints[d, k].astype(jnp.float32)
            fixed[d] = total

    eye = iota((NB2, NB2), 0) == iota((NB2, NB2), 1)
    zero = jnp.zeros((NB2, NB2), jnp.bfloat16)

    def accumulate(first, count):
        both = jnp.concatenate([jnp.concatenate([packed[0], zero], axis=1),
                                jnp.concatenate([zero, packed[1]], axis=1)], axis=0)
        sums = [fock[0], fock[1]]
        for g in range(count // PART):
            at = pl.ds(first + g * PART, PART)
            parts = [ri[d, at] for d in range(2)]
            wide = jnp.concatenate([p.reshape(PART * NB2, NB2) for p in parts], axis=1)
            half = jnp.dot(wide, both, preferred_element_type=jnp.float32)
            rows = []
            for d in range(2):
                squares = []
                for i in range(PART):
                    square = half[i * NB2:(i + 1) * NB2, d * NB2:(d + 1) * NB2]
                    fit = (parts[d][i] * packed[d]).astype(jnp.float32).reshape(-1, 8, NB2)
                    fit = jnp.sum(jnp.sum(fit, axis=0), axis=0, keepdims=True)
                    fit = jnp.sum(fit, axis=1, keepdims=True)
                    fit = -2.0 * fit.astype(jnp.bfloat16).astype(jnp.float32)
                    squares.append(jnp.where(eye, square + fit, square).astype(jnp.bfloat16))
                rows.append(jnp.concatenate(squares, axis=1))
            out = jnp.dot(jnp.concatenate(rows, axis=0), wide, preferred_element_type=jnp.float32)
            sums[0] = sums[0] + out[:NB2, :NB2]
            sums[1] = sums[1] + out[NB2:, NB2:]
        fock[0] = sums[0]
        fock[1] = sums[1]

    def begin():
        packed[...] = dens[...].astype(jnp.bfloat16)
        fock[...] = jnp.zeros_like(fock)

    def update():
        for d in range(2):
            matrix = fixed[d] - 0.5 * fock[d]
            fock[d] = matrix
            dens[d] = start[d] - damping * dot32(dot32(start[d], matrix), start[d])

    begin()

    def arriving(c, carry):
        load(c, 0).wait()
        load(c, 1).wait()

        @pl.when(c + 1 < CHUNKS)
        def _():
            load_chunk(c + 1)

        @pl.when(c == CHUNKS - 1)
        def _():
            for copy in late:
                copy.start()

        accumulate(c * per_chunk, per_chunk)
        return carry

    lax.fori_loop(0, CHUNKS, arriving, 0)
    for copy in late:
        copy.wait()
    fill_fixed()
    update()

    def sweep(t, carry):
        begin()

        def body(step, inner_carry):
            accumulate(step * STEP, STEP)
            return inner_carry

        lax.fori_loop(0, NAUX // STEP, body, 0)
        update()
        return carry

    lax.fori_loop(1, ITERS, sweep, 0)

    for d in range(2):
        matrix, density = fock[d], dens[d]
        energy[d] = (0.5 / NB2) * jnp.sum(density * (core_ham[d] + matrix))
        block = dot32(dot32(density, matrix), density)
        weighted[d] = jnp.where(left, block[:NB], block[NB:])
    for j in range(N_INNER):
        for d in range(2):
            blocks[j, d] = weighted[d, j * 8:(j + 1) * 8]


def route_kernel(pairs, got, out, count, owners, ranks):
    group = lax.axis_index("group")
    for o in range(N_GROUP):
        count[o] = 0
    for side in range(2):
        for dimer in range(DIM_GRP):
            owner = owner_of(pairs[side, group * DIM_GRP + dimer])
            rank = count[owner]
            owners[2 * dimer + side] = owner
            ranks[2 * dimer + side] = rank
            count[owner] = rank + 1
    out[...] = jnp.zeros_like(out)
    lane_half = iota((8, 128), 1) // NB
    for dimer in range(DIM_GRP):
        block = got[dimer // 2, dimer % 2]
        turned = pltpu.roll(block, NB, 1)
        for side in range(2):
            owner, rank = owners[2 * dimer + side], ranks[2 * dimer + side]
            half = lax.rem(rank, 2)
            value = jnp.where(half == side, block, turned)
            here = (owner, lax.div(rank, 2))
            out[here] = jnp.where(lane_half == half, value, out[here])


def home_kernel(table, got, out):
    out[...] = jnp.zeros_like(out)
    for g in range(N_GROUP):
        for s in range(CAP):
            at = table[s, g]
            block = got[g, s // 2]
            value = block[:, :NB] if s % 2 == 0 else pltpu.roll(block, NB, 1)[:, :NB]
            out[at] = out[at] + jnp.where(s < table[CAP, g], value, 0.0)


def params(mib):
    return pltpu.CompilerParams(vmem_limit_bytes=mib * 1024 * 1024)


def per_device(densities, ref_charge, site_pos, dimer_pairs, probe_pos, core_ham, probe_ints, ri_ints):
    f32, i32 = jnp.float32, jnp.int32
    pairs = dimer_pairs.T
    swap = [(i, i ^ 1) for i in range(N_INNER)]

    with jax.named_scope("pack"):
        send, table = pl.pallas_call(
            pack_kernel,
            out_shape=(jax.ShapeDtypeStruct((N_GROUP, ROWS, 128), f32),
                       jax.ShapeDtypeStruct((8, 128), i32)),
            in_specs=[VMEM, ANY, VMEM, VMEM],
            out_specs=(VMEM, VMEM),
            scratch_shapes=[pltpu.VMEM((FRAG_GRP, NB, NB), f32), pltpu.SMEM((8, 128), i32),
                            pltpu.SemaphoreType.DMA, pltpu.SemaphoreType.DMA],
            compiler_params=params(58),
            name="pack",
        )(pairs, densities, ref_charge.T, site_pos)
    mine = lax.all_to_all(send, "group", split_axis=0, concat_axis=0, tiled=True)
    other = lax.ppermute(mine, "inner", swap)

    with jax.named_scope("scf"):
        square = pltpu.VMEM((2, NB2, NB2), f32)
        blocks, energy = pl.pallas_call(
            scf_kernel,
            out_shape=(jax.ShapeDtypeStruct((N_INNER, 2, 8, 128), f32), jax.ShapeDtypeStruct((2,), f32)),
            in_specs=[SMEM, VMEM, SMEM, ANY, ANY, ANY, ANY, ANY],
            out_specs=(VMEM, SMEM),
            scratch_shapes=[
                pltpu.VMEM((2, NAUX, NB2, NB2), jnp.bfloat16),
                square, square, square,
                pltpu.VMEM((2, NB2, NB2), jnp.bfloat16),
                square,
                pltpu.VMEM((2, NB, NB2), f32),
                pltpu.VMEM((4, TRI, 128), f32),
                pltpu.VMEM((2, N_GROUP, ROWS - TRI, 128), f32),
                square,
                pltpu.VMEM((2, NPROBE, NB2, NB2), jnp.bfloat16),
                pltpu.SemaphoreType.DMA((CHUNKS, 2)),
                pltpu.SemaphoreType.DMA((4,)),
                pltpu.SemaphoreType.DMA((4,)),
            ],
            compiler_params=params(58),
            name="scf",
        )(pairs, pairs, probe_pos, mine, other, core_ham, probe_ints, ri_ints)
    rows = lax.all_to_all(blocks, "inner", split_axis=0, concat_axis=0, tiled=True)

    with jax.named_scope("route"):
        slots = pl.pallas_call(
            route_kernel,
            out_shape=jax.ShapeDtypeStruct((N_GROUP, CAP // 2, 8, 128), f32),
            in_specs=[SMEM, VMEM],
            out_specs=VMEM,
            scratch_shapes=[pltpu.SMEM((N_GROUP,), i32), pltpu.SMEM((2 * DIM_GRP,), i32),
                            pltpu.SMEM((2 * DIM_GRP,), i32)],
            name="route",
        )(pairs, rows)
    homed = lax.all_to_all(slots, "group", split_axis=0, concat_axis=0, tiled=True)

    with jax.named_scope("home"):
        frag_weight = pl.pallas_call(
            home_kernel,
            out_shape=jax.ShapeDtypeStruct((FRAG_GRP, 8, NB), f32),
            in_specs=[SMEM, VMEM],
            out_specs=VMEM,
            name="home",
        )(table, homed)
    return (frag_weight, energy)


def solution(mesh):
    in_specs = (
        P("group", None, None),
        P("group", None),
        P(None, "group"),
        P(),
        P(None, ("group", "inner")),
        P(("group", "inner"), None, None),
        P(("group", "inner"), None, None, None),
        P(("group", "inner"), None, None, None),
    )
    out_specs = (P("group", "inner", None), P(("group", "inner")))
    return jax.shard_map(
        per_device, mesh=mesh, in_specs=in_specs, out_specs=out_specs, check_vma=False
    )
```
